128 devices in a mesh: row: 8 (over z_lo, y), col: 16 (over x, z_hi, core).
Axes of the slice: x: 4, y: 4, z: 4 (z_hi: 2, z_lo: 2; z = z_hi * 2 + z_lo), core: 2. Of those that a mesh axis runs over, the one named last changes fastest.
Arguments:
- features: bfloat16 [32768, 512], P(('row', 'col')), may hold values from -6 to 6
- weight: bfloat16 [512, 512], replicated, may hold values from -0.25 to 0.25
- cotangent: bfloat16 [32768, 512], P(('row', 'col')), may hold values from -6 to 6
- tile_coords: int32 [8, 16, 192, 2], P('row', 'col'), may hold values from 0 to 31, as said below
- tile_values: bfloat16 [8, 16, 192, 128, 128], P('row', 'col'), may hold values from -0.09375 to 0.09375
- tile_count: int32 [8, 16], P('row', 'col'), may hold values from 24 to 192, as said below
Outputs:
- output: bfloat16 [32768, 512], P(('row', 'col'))
- features_grad: bfloat16 [32768, 512], P(('row', 'col'))
- weight_grad: float32 [512, 512], replicated
The draws below stay inside these ranges and needn't reach their ends.
Inputs may be any that keep to these rules, and one draw needn't show every extreme that they name: `tile_coords`: within one device the slots name distinct tiles, and each of its 32 tile rows is named by exactly 6 slots; tile columns lie below 16. `tile_count`: exactly one device in each draw has all 192 slots live.
All inputs are finite; a program needn't handle non-finite values.
Results may differ from the reference program's by a relative error of at most 0.023.
Values may be sent and summed in bfloat16 or wider, within the bound.
No kernel may reach another device: no remote copies, remote signals or barrier semaphores. Data moves between devices by JAX's collectives and lax.ppermute only.
A program may use at most 128 MiB of HBM per device.

```python
import jax
import jax.numpy as jnp
from jax import lax

FEAT = 512
TILE = 128
SPAN_DEV = 256
TILES_PER_ROW = 6
GRID_ROWS = 8
GRID_COLS = 16
ROW_TILES = 32
COL_TILES = 16
SLOTS = 192
NODES = 32768


def draw_tile_coords(key, part):
    key = jax.random.fold_in(key, 11)
    key_cols, key_order = jax.random.split(key)
    devices = GRID_ROWS * GRID_COLS
    col_scores = jax.random.randint(key_cols, (devices, ROW_TILES, COL_TILES), 0, 2 ** 20) * COL_TILES
    col_scores = col_scores + jnp.arange(COL_TILES, dtype=jnp.int32)
    chosen = jnp.argsort(col_scores, axis=-1)[:, :, :TILES_PER_ROW].astype(jnp.int32)
    rows = jnp.broadcast_to(jnp.arange(ROW_TILES, dtype=jnp.int32)[None, :, None], chosen.shape)
    rows = rows.reshape(devices, SLOTS)
    cols = chosen.reshape(devices, SLOTS)
    order_scores = jax.random.randint(key_order, (devices, SLOTS), 0, 2 ** 20) * SLOTS
    order_scores = order_scores + jnp.arange(SLOTS, dtype=jnp.int32)
    order = jnp.argsort(order_scores, axis=-1)
    rows = jnp.take_along_axis(rows, order, axis=-1)
    cols = jnp.take_along_axis(cols, order, axis=-1)
    return jnp.stack([rows, cols], axis=-1).reshape(GRID_ROWS, GRID_COLS, SLOTS, 2).astype(jnp.int32)


def draw_tile_count(key, part):
    key = jax.random.fold_in(key, 12)
    key_counts, key_full = jax.random.split(key)
    counts = jax.random.randint(key_counts, (GRID_ROWS * GRID_COLS,), SLOTS // 8, SLOTS // 2 + 1)
    full_device = jax.random.randint(key_full, (), 0, GRID_ROWS * GRID_COLS)
    counts = jnp.where(jnp.arange(GRID_ROWS * GRID_COLS, dtype=jnp.int32) == full_device, SLOTS, counts)
    return counts.reshape(GRID_ROWS, GRID_COLS).astype(jnp.int32)


def levels(stream_key, dims, cuts, least, high):
    def one(position, shards_of):
        draws = jax.random.uniform(jax.random.fold_in(jax.random.fold_in(stream_key, 6), position), (shards_of,), jnp.float32, least / len(cuts), high / len(cuts))
        return jnp.repeat(jnp.exp(draws), dims[position] // shards_of).reshape((-1,) + (1,) * (len(dims) - position - 1))

    factor_of = one(*cuts[0])
    for cut in cuts[1:]:
        factor_of = factor_of * one(*cut)
    return factor_of


def centred(own_key, shape, scale, bound, cuts=(), kind=jnp.bfloat16):
    factor_of = levels(own_key, shape, cuts, -0.22, 0.18) if cuts else 1.0
    drawn = jax.random.normal(own_key, shape, jnp.float32) * scale * factor_of
    return jnp.minimum(jnp.maximum(drawn, -bound), bound).astype(kind)


def setup_inputs(seed: int = 0) -> dict:
    splits = jax.random.split(jax.random.key(seed), 7)
    return {
        "features": centred(splits[0], (NODES, FEAT), 1.0, 6.0, ((0, 128),)),
        "weight": centred(splits[1], (FEAT, FEAT), FEAT ** -0.5, 0.25),
        "cotangent": centred(splits[2], (NODES, FEAT), 1.0, 6.0, ((0, 128),)),
        "tile_coords": draw_tile_coords(jax.random.fold_in(splits[6], 71), 0),
        "tile_values": centred(splits[4], (GRID_ROWS, GRID_COLS, SLOTS, TILE, TILE), ((TILE * TILES_PER_ROW * GRID_COLS // 3) ** -0.5), 0.09375, ((0, 8), (1, 16))),
        "tile_count": draw_tile_count(jax.random.fold_in(splits[6], 71), 0),
    }


def block_sum(values, coords, count, tiles, src_pick, dst_pick, out_tiles, form):
    width = tiles.shape[-1]
    total = jnp.zeros((out_tiles, TILE, width), jnp.float32)

    def add_group(group_index, total):
        start = group_index * 32
        vals = lax.dynamic_slice_in_dim(values, start, 32, 0).astype(jnp.float32)
        crd = lax.dynamic_slice_in_dim(coords, start, 32, 0)
        picked = tiles[crd[:, src_pick]].astype(jnp.float32)
        prod = jnp.einsum(form, vals, picked)
        live = (start + jnp.arange(32, dtype=jnp.int32) < count)[:, None, None]
        return total.at[crd[:, dst_pick]].add(jnp.where(live, prod, jnp.zeros_like(prod)))

    return lax.fori_loop(0, (count + 31) // 32, add_group, total)


def rounded(part):
    return lax.optimization_barrier(part.astype(jnp.bfloat16)).astype(jnp.float32)


def reference(features, weight, cotangent, tile_coords, tile_values, tile_count):
    width = features.shape[1]
    projected = jnp.dot(features, weight, preferred_element_type=jnp.float32).astype(jnp.bfloat16)
    grid_nodes = projected.reshape(GRID_ROWS, GRID_COLS, SPAN_DEV, width)
    cot_panels = cotangent.reshape(GRID_ROWS, GRID_COLS * SPAN_DEV, width)

    def forward_device(device, acc):
        r = device // GRID_COLS
        c = device % GRID_COLS
        panel = lax.dynamic_index_in_dim(grid_nodes, c, 1, keepdims=False).reshape(COL_TILES, TILE, width)
        part = block_sum(tile_values[r, c], tile_coords[r, c], tile_count[r, c], panel, 1, 0, ROW_TILES, "sij,sjf->sif")
        return acc.at[r].add(rounded(part.reshape(ROW_TILES * TILE, width)))

    acc = jnp.zeros((GRID_ROWS, ROW_TILES * TILE, width), jnp.float32)
    acc = lax.fori_loop(0, GRID_ROWS * GRID_COLS, forward_device, acc)
    output = acc.reshape(NODES, width).astype(jnp.bfloat16)

    def backward_device(device, acc):
        r = device // GRID_COLS
        c = device % GRID_COLS
        panel = lax.dynamic_index_in_dim(cot_panels, r, 0, keepdims=False).reshape(ROW_TILES, TILE, width)
        part = block_sum(tile_values[r, c], tile_coords[r, c], tile_count[r, c], panel, 0, 1, COL_TILES, "sji,sjf->sif")
        return acc.at[:, c].add(rounded(part.reshape(GRID_ROWS, SPAN_DEV, width)))

    back = jnp.zeros((GRID_ROWS, GRID_COLS, SPAN_DEV, width), jnp.float32)
    back = lax.fori_loop(0, GRID_ROWS * GRID_COLS, backward_device, back)
    agg_grad = back.reshape(NODES, width).astype(jnp.bfloat16)
    features_grad = jnp.dot(agg_grad, weight.T, preferred_element_type=jnp.float32).astype(jnp.bfloat16)
    weight_grad = jnp.dot(features.T, agg_grad, preferred_element_type=jnp.float32) * (NODES ** -0.5)
    return output, features_grad, weight_grad
```

```python
import functools

import jax
import jax.numpy as jnp
from jax import lax
from jax.experimental import pallas as pl
from jax.experimental.pallas import tpu as pltpu
from jax.sharding import PartitionSpec as P

TILE = 128
SPAN = 256
FEAT = 512
PER_ROW = 6
ROW_TILES = 32
COL_TILES = 16
SLOTS = 192
CHUNK = 6
ROW_STEP = 4
CHUNK_STEP = 4
MAX_CHUNKS = 64
BF16 = jnp.bfloat16
F32 = jnp.float32
SMEM = pl.BlockSpec(memory_space=pltpu.SMEM)
VMEM = pl.BlockSpec(memory_space=pltpu.VMEM)


def flat(x, y, z, core):
    return ((z % 2) * 4 + y % 4) * 16 + (x % 4) * 4 + (z // 2) * 2 + core


def permute(value, step):
    pairs = [
        (flat(x, y, z, c), flat(*step(x, y, z, c)))
        for x in range(4)
        for y in range(4)
        for z in range(4)
        for c in range(2)
    ]
    return lax.ppermute(value, ("row", "col"), pairs)


def to_core(x, y, z, c):
    return x, y, z, 1 - c


def to_z_near(x, y, z, c):
    return x, y, z ^ 1, c


def to_z_far(x, y, z, c):
    return x, y, z ^ 2, c


def along_x(k):
    return lambda x, y, z, c: (x + k, y, z, c)


def along_y(k):
    return lambda x, y, z, c: (x, y + k, z, c)


def block(i):
    return pl.ds(pl.multiple_of(i * TILE, TILE), TILE)


def ring_place(distance):
    return jnp.where(distance == 0, 0, jnp.where(distance == 3, 1, distance + 1))


def lists_kernel(coords, count, row_slot, row_col, chunk_col, chunk_slot, chunk_row, n_chunks, row_fill, col_fill, col_chunk):
    row, col = lax.axis_index("row"), lax.axis_index("col")
    my_y, my_near = row % 4, row // 4
    my_x, my_far, my_core = col // 4, (col // 2) % 2, col % 2
    live = count[0, 0]

    def col_place(b):
        owner = b // 2
        place = ring_place((owner % 4 - my_y + 4) % 4) * 2 + (owner // 4 + my_near) % 2
        return place * 2 + b % 2

    def place_of_row(a):
        owner = a // 2
        place = ((owner % 2 + my_core) % 2) * 8 + ring_place((owner // 4 - my_x + 4) % 4) * 2
        return (place + ((owner // 2) % 2 + my_far) % 2) * 2 + a % 2

    def clear_row(a, carry):
        row_fill[a] = 0
        return carry

    def clear_col(b, carry):
        col_fill[b] = CHUNK
        col_chunk[b] = 0
        return carry

    lax.fori_loop(0, ROW_TILES, clear_row, 0)
    lax.fori_loop(0, COL_TILES, clear_col, 0)

    def slot(s, used):
        a = place_of_row(coords[0, 0, s, 0])
        b = col_place(coords[0, 0, s, 1])
        n = row_fill[a]
        row_fill[a] = n + 1
        is_live = s < live
        row_slot[a * PER_ROW + n] = jnp.where(is_live, s, -1)
        row_col[a * PER_ROW + n] = b
        m = col_fill[b]
        opens = jnp.logical_and(is_live, m == CHUNK)

        @pl.when(opens)
        def _():
            col_chunk[b] = used
            chunk_col[used] = b
            for i in range(CHUNK):
                chunk_slot[used * CHUNK + i] = -1
                chunk_row[used * CHUNK + i] = 0

        @pl.when(is_live)
        def _():
            k = jnp.where(opens, 0, m)
            place = col_chunk[b] * CHUNK + k
            chunk_slot[place] = s
            chunk_row[place] = a
            col_fill[b] = k + 1

        return jnp.where(opens, used + 1, used)

    used = lax.fori_loop(0, SLOTS, slot, 0)
    n_chunks[0] = (used + CHUNK_STEP - 1) // CHUNK_STEP
    for k in range(CHUNK_STEP):
        chunk_col[used + k] = 0
        for i in range(CHUNK):
            chunk_slot[(used + k) * CHUNK + i] = -1
            chunk_row[(used + k) * CHUNK + i] = 0


def make_lists(coords, count):
    def ints(n):
        return jax.ShapeDtypeStruct((n,), jnp.int32)

    return pl.pallas_call(
        lists_kernel,
        out_shape=(
            ints(SLOTS),
            ints(SLOTS),
            ints(MAX_CHUNKS),
            ints(MAX_CHUNKS * CHUNK),
            ints(MAX_CHUNKS * CHUNK),
            ints(1),
        ),
        in_specs=[SMEM, SMEM],
        out_specs=(SMEM,) * 6,
        scratch_shapes=[pltpu.SMEM((ROW_TILES,), jnp.int32), pltpu.SMEM((COL_TILES,), jnp.int32), pltpu.SMEM((COL_TILES,), jnp.int32)],
    )(coords, count)


def live_tile(values, slot):
    tile = values[jnp.maximum(slot, 0)]
    return tile * jnp.where(slot >= 0, 1.0, 0.0).astype(BF16)


def tiles_kernel(row_slot, row_col, chunk_col, chunk_slot, chunk_row, n_chunks, values, feats, cots, rows_out, cols_out, total):
    def row_step(q, carry):
        for k in range(ROW_STEP):
            a = q * ROW_STEP + k
            tiles = [live_tile(values, row_slot[a * PER_ROW + i]) for i in range(PER_ROW)]
            source = [feats[block(row_col[a * PER_ROW + i]), :] for i in range(PER_ROW)]
            rows_out[block(a), :] = jnp.dot(
                jnp.concatenate(tiles, axis=1), jnp.concatenate(source, axis=0), preferred_element_type=F32
            ).astype(BF16)
        return carry

    lax.fori_loop(0, ROW_TILES // ROW_STEP, row_step, 0)
    total[...] = jnp.zeros_like(total)

    def chunk_step(q, carry):
        products = []
        for k in range(CHUNK_STEP):
            first = (q * CHUNK_STEP + k) * CHUNK
            tiles = [live_tile(values, chunk_slot[first + i]) for i in range(CHUNK)]
            source = [cots[block(chunk_row[first + i]), :] for i in range(CHUNK)]
            products.append(
                lax.dot_general(
                    jnp.concatenate(tiles, axis=0),
                    jnp.concatenate(source, axis=0),
                    (((0,), (0,)), ((), ())),
                    preferred_element_type=F32,
                )
            )
        for k in range(CHUNK_STEP):
            total[block(chunk_col[q * CHUNK_STEP + k]), :] += products[k]
        return carry

    lax.fori_loop(0, n_chunks[0], chunk_step, 0)
    cols_out[...] = total[...].astype(BF16)


def tile_sums(lists, values, feats, cots):
    return pl.pallas_call(
        tiles_kernel,
        out_shape=(
            jax.ShapeDtypeStruct((ROW_TILES * TILE, FEAT), BF16),
            jax.ShapeDtypeStruct((COL_TILES * TILE, FEAT), BF16),
        ),
        in_specs=[SMEM] * 6 + [VMEM] * 3,
        out_specs=(VMEM, VMEM),
        scratch_shapes=[pltpu.VMEM((COL_TILES * TILE, FEAT), F32)],
        compiler_params=pltpu.CompilerParams(vmem_limit_bytes=40 * 2**20),
    )(*lists, values, feats, cots)


def stack(*parts):
    return jnp.concatenate(parts, axis=0)


def add(*parts):
    total = parts[0].astype(F32)
    for part in parts[1:]:
        total = total + part.astype(F32)
    return total.astype(BF16)


def gather(own, near, ring):
    pair = stack(own, permute(own, near))
    before, after = permute(pair, ring(1)), permute(pair, ring(-1))
    far = stack(permute(before[:SPAN], ring(1)), permute(after[SPAN:], ring(-1)))
    return stack(pair, before, after, far)


def scatter(parts, near, ring):
    own, before, after, far = (parts[i * 2 * SPAN : (i + 1) * 2 * SPAN] for i in range(4))
    to_after = permute(far[:SPAN], ring(1))
    to_before = permute(far[SPAN:], ring(-1))
    from_before = permute(stack(add(after[:SPAN], to_after), after[SPAN:]), ring(1))
    from_after = permute(stack(before[:SPAN], add(before[SPAN:], to_before)), ring(-1))
    passed = permute(add(own[SPAN:], from_before[SPAN:], from_after[SPAN:]), near)
    return add(own[:SPAN], from_before[:SPAN], from_after[:SPAN], passed)


def per_device(features, weight, cotangent, tile_coords, tile_values, tile_count):
    values = tile_values[0, 0]
    lists = make_lists(tile_coords, tile_count)
    feats = gather(features, to_z_near, along_y)
    half = gather(cotangent, to_z_far, along_x)
    cots = stack(half, permute(half, to_core))
    row_part, col_part = tile_sums(lists, values, feats, cots)
    term = lax.dot_general(feats, col_part, (((0,), (0,)), ((), ())), preferred_element_type=F32).astype(BF16)
    mine, other = row_part[: 8 * SPAN], row_part[8 * SPAN :]
    aggregated = scatter(add(mine, permute(other, to_core)), to_z_far, along_x)
    agg_grad = scatter(col_part, to_z_near, along_y)
    output = jnp.dot(aggregated, weight, preferred_element_type=F32).astype(BF16)
    features_grad = lax.dot_general(agg_grad, weight, (((1,), (1,)), ((), ())), preferred_element_type=F32).astype(BF16)
    devices = lax.axis_size("row") * lax.axis_size("col")
    pieces = lax.all_to_all(term.reshape(devices, FEAT // devices, FEAT), ("row", "col"), 0, 0)
    piece = jnp.sum(pieces.astype(F32), axis=0).astype(BF16)
    spread = jnp.broadcast_to(piece[None], (devices,) + piece.shape)
    whole = lax.all_to_all(spread, ("row", "col"), 0, 0)
    weight_grad = whole.reshape(FEAT, FEAT).astype(F32) * (devices * SPAN) ** (-0.5)
    return output, features_grad, weight_grad


def solution(mesh):
    return jax.shard_map(
        per_device,
        mesh=mesh,
        in_specs=(
            P(("row", "col"), None),
            P(),
            P(("row", "col"), None),
            P("row", "col", None, None),
            P("row", "col", None, None, None),
            P("row", "col"),
        ),
        out_specs=(P(("row", "col"), None), P(("row", "col"), None), P()),
        check_vma=False,
    )
```

```python
import functools

import jax
import jax.numpy as jnp
from jax import lax
from jax.experimental import pallas as pl
from jax.experimental.pallas import tpu as pltpu
from jax.sharding import PartitionSpec as P

TILE = 128
SPAN = 256
FEAT = 512
PER_ROW = 6
SLOTS = 192
CHUNK = 6
STEP = 4
WIDE = 384
PART = 64
HALF_ROWS = 8 * SPAN
BF16 = jnp.bfloat16
F32 = jnp.float32
SMEM = pl.BlockSpec(memory_space=pltpu.SMEM)
VMEM = pl.BlockSpec(memory_space=pltpu.VMEM)
DISTANCE = (0, 3, 1, 2)


def flat(x, y, z, core):
    return ((z % 2) * 4 + y % 4) * 16 + (x % 4) * 4 + (z // 2) * 2 + core


def permute(value, step):
    pairs = [
        (flat(x, y, z, c), flat(*step(x, y, z, c)))
        for x in range(4)
        for y in range(4)
        for z in range(4)
        for c in range(2)
    ]
    return lax.ppermute(value, ("row", "col"), pairs)


def to_core(x, y, z, c):
    return x, y, z, 1 - c


def ring(k):
    return lambda x, y, z, c: (x, y + k, z, c) if c == 0 else (x + k, y, z, c)


def to_z(x, y, z, c):
    return x, y, z ^ (1 if c == 0 else 2), c


def cross_ring(k):
    return lambda x, y, z, c: (x + k, y, z, c) if c == 0 else (x, y + k, z, c)


def along_z(k):
    return lambda x, y, z, c: (x, y, (z + k) % 4, c)


def rows(first, count):
    return pl.ds(pl.multiple_of(first, count), count)


def block(i):
    return rows(i * TILE, TILE)


def ring_place(distance):
    return jnp.where(distance == 0, 0, jnp.where(distance == 3, 1, distance + 1))


def coordinates():
    row, col = lax.axis_index("row"), lax.axis_index("col")
    return col // 4, row % 4, row // 4, (col // 2) % 2, col % 2


def part_at(place):
    near, far = coordinates()[2:4]
    return (far * 2 + near + DISTANCE[place]) % 4


def lists_kernel(coords, count, lists):
    my_x, my_y, my_near, my_far, my_core = coordinates()
    live = count[0, 0]
    sublane = lax.broadcasted_iota(jnp.int32, (SLOTS, SLOTS), 0)
    lane = lax.broadcasted_iota(jnp.int32, (SLOTS, SLOTS), 1)
    wide = lax.broadcasted_iota(jnp.int32, (SLOTS, WIDE), 1)
    same = sublane == lane

    def picked(mask, value):
        return jnp.where(mask, value, 0.0)

    def column(line):
        return jnp.sum(picked(same, line.astype(F32)), axis=1, keepdims=True).astype(jnp.int32)

    row_line, col_line = coords[0:1, :], coords[1:2, :]
    a, b = column(row_line), column(col_line)
    a_owner, b_owner = a >> 1, b >> 1
    a_place = (1 - (((a_owner >> 1) & 1) ^ my_far)) * 4 + ring_place(((a_owner >> 2) - my_x) & 3)
    b_place = (1 - ((b_owner >> 2) ^ my_near)) * 4 + ring_place(((b_owner & 3) - my_y) & 3)
    a_from, b_from = a_place ^ 4, b_place ^ 4
    a_tile = a_place * 4 + (a_owner & 1) * 2 + (a & 1)
    b_tile = b_place * 2 + (b & 1)
    a_source = a_from * 4 + (a_owner & 1) * 2 + (a & 1) + (1 - my_core) * 32
    b_source = b_from * 4 + my_core * 2 + (b & 1) + my_core * 32
    slot = sublane[:, 0:1]
    is_live = slot < live

    row_rank = jnp.sum(picked((a == row_line) & (lane < sublane), 1.0), axis=1, keepdims=True).astype(jnp.int32)
    at_row = wide == a_tile * PER_ROW + row_rank
    named = jnp.where(is_live, slot, -1).astype(F32)
    lists[0:1, :] = jnp.sum(picked(at_row, named), axis=0, keepdims=True).astype(jnp.int32)
    lists[1:2, :] = jnp.sum(picked(at_row, b_source.astype(F32)), axis=0, keepdims=True).astype(jnp.int32)

    earlier = (b == col_line) & (lane < sublane) & (lane < live)
    col_rank = jnp.sum(picked(earlier, 1.0), axis=1, keepdims=True).astype(jnp.int32)
    filled = jnp.sum(picked((b_tile == wide) & is_live, 1.0), axis=0, keepdims=True).astype(jnp.int32)
    chunks = ((filled + (CHUNK - 1)) * 43) >> 8
    used = jnp.sum(chunks.astype(F32), axis=1, keepdims=True).astype(jnp.int32)
    base = jnp.sum(picked(wide < b_tile, chunks.astype(F32)), axis=1, keepdims=True).astype(jnp.int32)
    which = (col_rank * 43) >> 8
    chunk = base + which
    place = col_rank - which * CHUNK
    at_chunk = (wide == chunk * CHUNK + place) & is_live
    opens = (wide == chunk) & is_live & (place == 0)
    lists[2:3, :] = jnp.sum(picked(at_chunk, (slot + 1).astype(F32)), axis=0, keepdims=True).astype(jnp.int32) - 1
    lists[3:4, :] = jnp.sum(picked(at_chunk, a_source.astype(F32)), axis=0, keepdims=True).astype(jnp.int32)
    lists[4:5, :] = jnp.sum(picked(opens, b_tile.astype(F32)), axis=0, keepdims=True).astype(jnp.int32)
    lists[5:6, :] = jnp.broadcast_to((used + (STEP - 1)) >> 2, (1, WIDE))
    lists[6:8, :] = jnp.zeros((2, WIDE), jnp.int32)


def make_lists(coords, count):
    return pl.pallas_call(
        lists_kernel,
        out_shape=jax.ShapeDtypeStruct((8, WIDE), jnp.int32),
        in_specs=[VMEM, SMEM],
        out_specs=VMEM,
        compiler_params=pltpu.CompilerParams(vmem_limit_bytes=12 * 2**20),
    )(coords, count)


def live_tile(values, slot):
    tile = values[jnp.maximum(slot, 0)]
    return tile * jnp.where(slot >= 0, 1.0, 0.0).astype(BF16)


def backward_kernel(lists, values, panels, far, near, term_keep, term_send, total, whole, term):
    core = coordinates()[4]
    total[...] = jnp.zeros_like(total)

    def chunk_step(q, carry):
        products = []
        for k in range(STEP):
            first = (q * STEP + k) * CHUNK
            tiles = [live_tile(values, lists[2, first + i]) for i in range(CHUNK)]
            source = [panels[block(lists[3, first + i]), :] for i in range(CHUNK)]
            products.append(
                lax.dot_general(
                    jnp.concatenate(tiles, axis=0),
                    jnp.concatenate(source, axis=0),
                    (((0,), (0,)), ((), ())),
                    preferred_element_type=F32,
                )
            )
        for k in range(STEP):
            total[block(lists[4, q * STEP + k]), :] += products[k]
        return carry

    lax.fori_loop(0, lists[5, 0], chunk_step, 0)
    whole[...] = total[...].astype(BF16)
    for half, target in ((0, far), (1, near)):
        for q in range(4):
            from_here = (half * 4 + q) * SPAN
            target[rows(q * 2 * SPAN + core * SPAN, SPAN), :] = whole[from_here : from_here + SPAN, :]
            target[rows(q * 2 * SPAN + (1 - core) * SPAN, SPAN), :] = jnp.zeros((SPAN, FEAT), BF16)
    start = core * 16 * SPAN + core * SPAN
    feats = jnp.concatenate([panels[rows(start + (q ^ 4) * 2 * SPAN, SPAN), :] for q in range(8)], axis=0)
    term[...] = lax.dot_general(
        feats, whole[...], (((0,), (0,)), ((), ())), preferred_element_type=F32
    ).astype(BF16)
    for place in range(4):
        for target, side in ((term_keep, core), (term_send, 1 - core)):
            first = side * SPAN + part_at(place) * PART
            target[place * PART : (place + 1) * PART, :] = term[rows(first, PART), :]


def forward_kernel(half, lists, values, panels, back, keep, send):
    core = coordinates()[4]

    def row_step(q, carry):
        products = []
        for k in range(STEP):
            first = (half * 16 + q * STEP + k) * PER_ROW
            tiles = [live_tile(values, lists[0, first + i]) for i in range(PER_ROW)]
            source = [panels[block(lists[1, first + i]), :] for i in range(PER_ROW)]
            products.append(
                jnp.dot(
                    jnp.concatenate(tiles, axis=1), jnp.concatenate(source, axis=0), preferred_element_type=F32
                ).astype(BF16)
            )
        here = rows(q * STEP * TILE, STEP * TILE)

        @pl.when(core == half)
        def _():
            send[here, :] = jnp.concatenate(products, axis=0)
            keep[here, :] = back[here, :]

        @pl.when(core == 1 - half)
        def _():
            keep[here, :] = jnp.concatenate(products, axis=0)
            send[here, :] = back[here, :]

        return carry

    lax.fori_loop(0, 16 // STEP, row_step, 0)


def shape(n, dtype=BF16):
    return jax.ShapeDtypeStruct((n, FEAT), dtype)


def backward_sums(lists, values, panels):
    return pl.pallas_call(
        backward_kernel,
        out_shape=(shape(HALF_ROWS), shape(HALF_ROWS), shape(SPAN), shape(SPAN)),
        in_specs=[SMEM, VMEM, VMEM],
        out_specs=[VMEM] * 4,
        scratch_shapes=[
            pltpu.VMEM((8 * SPAN, FEAT), F32),
            pltpu.VMEM((8 * SPAN, FEAT), BF16),
            pltpu.VMEM((FEAT, FEAT), BF16),
        ],
        compiler_params=pltpu.CompilerParams(vmem_limit_bytes=12 * 2**20),
    )(lists, values, panels)


def forward_sums(half, lists, values, panels, back):
    return pl.pallas_call(
        functools.partial(forward_kernel, half),
        out_shape=(shape(HALF_ROWS), shape(HALF_ROWS)),
        in_specs=[SMEM, VMEM, VMEM, VMEM],
        out_specs=[VMEM] * 2,
        compiler_params=pltpu.CompilerParams(vmem_limit_bytes=8 * 2**20),
    )(lists, values, panels, back)


def finish_kernel(final, got, weight, output, grad):
    core = coordinates()[4]

    def both(summed, agg):
        output[...] = jnp.dot(summed, weight[...], preferred_element_type=F32).astype(BF16)
        grad[...] = lax.dot_general(
            agg, weight[...], (((1,), (1,)), ((), ())), preferred_element_type=F32
        ).astype(BF16)

    @pl.when(core == 0)
    def _():
        both(final[0:SPAN, :], got[...])

    @pl.when(core == 1)
    def _():
        both(got[...], final[SPAN : 2 * SPAN, :])


def finish(final, got, weight):
    return pl.pallas_call(
        finish_kernel,
        out_shape=(shape(SPAN), shape(SPAN)),
        in_specs=[VMEM] * 3,
        out_specs=(VMEM, VMEM),
        compiler_params=pltpu.CompilerParams(vmem_limit_bytes=8 * 2**20),
    )(final, got, weight)


def place_kernel(scale, mine, other, grad):
    core = coordinates()[4]
    for place in range(4):
        for source, side in ((mine, core), (other, 1 - core)):
            first = side * SPAN + part_at(place) * PART
            grad[rows(first, PART), :] = source[place * PART : (place + 1) * PART, :].astype(F32) * scale


def place_parts(scale, mine, other):
    return pl.pallas_call(
        functools.partial(place_kernel, scale),
        out_shape=shape(FEAT, F32),
        in_specs=[VMEM, VMEM],
        out_specs=VMEM,
        compiler_params=pltpu.CompilerParams(vmem_limit_bytes=8 * 2**20),
    )(mine, other)


def stack(*parts):
    return jnp.concatenate(parts, axis=0)


def add(*parts):
    total = parts[0].astype(F32)
    for part in parts[1:]:
        total = total + part.astype(F32)
    return total.astype(BF16)


def ring_gather(own, step):
    opposite = permute(own, step(2))
    return own, permute(own, step(1)), permute(own, step(-1)), opposite


def ring_sum(pieces, step):
    own, before, after, opposite = pieces
    opposite = permute(opposite, step(2))
    return own, permute(after, step(1)), permute(before, step(-1)), opposite


def split(whole, size):
    return [whole[i * size : (i + 1) * size] for i in range(4)]


def per_device(features, weight, cotangent, tile_coords, tile_values, tile_count):
    values = tile_values[0, 0]
    lists = make_lists(jnp.transpose(tile_coords[0, 0]), tile_count)
    first = lax.axis_index("col") % 2 == 0
    other_features, other_cotangent = permute(features, to_core), permute(cotangent, to_core)
    own = jnp.where(first, stack(features, other_features), stack(other_cotangent, cotangent))
    from_z = permute(own, to_z)
    near = list(ring_gather(own, ring))
    from_z, *near, lists = lax.optimization_barrier((from_z, *near, lists))
    near = stack(*near, from_z)
    other_near = permute(near, to_core)
    far = stack(*ring_gather(from_z, ring)[1:])
    far, other_near = lax.optimization_barrier((far, other_near))
    panels = stack(near, far, other_near, permute(far, to_core))

    back_far, back_near, term_keep, term_send = backward_sums(lists, values, panels)
    part = add(term_keep, permute(term_send, to_core))
    part, back_far = lax.optimization_barrier((part, back_far))
    keep_far, send_far = forward_sums(0, lists, values, panels, back_far)
    sum_far = add(keep_far, permute(send_far, to_core))
    part = add(*ring_sum(split(part, PART), along_z))
    keep_near, send_near = forward_sums(1, lists, values, panels, back_near)
    sum_near = add(keep_near, permute(send_near, to_core))
    far = [stack(piece, part) for piece in split(sum_far, 2 * SPAN)]
    far = add(*ring_sum(far, ring))
    far, part = far[: 2 * SPAN], far[2 * SPAN :]
    near = add(*ring_sum([stack(piece, part) for piece in split(sum_near, 2 * SPAN)], cross_ring))
    near, part = near[: 2 * SPAN], near[2 * SPAN :]
    passed = permute(permute(far, to_z), to_core)
    mine = stack(*ring_gather(part, along_z))
    other = permute(mine, to_core)
    final = add(near, passed)
    got = permute(jnp.where(first, final[SPAN:], final[:SPAN]), to_core)
    output, features_grad = finish(final, got, weight)
    nodes = lax.axis_size("row") * lax.axis_size("col") * SPAN
    weight_grad = place_parts(nodes ** (-0.5), mine, other)
    return output, features_grad, weight_grad


def solution(mesh):
    return jax.shard_map(
        per_device,
        mesh=mesh,
        in_specs=(
            P(("row", "col"), None),
            P(),
            P(("row", "col"), None),
            P("row", "col", None, None),
            P("row", "col", None, None, None),
            P("row", "col"),
        ),
        out_specs=(P(("row", "col"), None), P(("row", "col"), None), P()),
        check_vma=False,
    )
```

```python
import functools

import jax
import jax.numpy as jnp
from jax import lax
from jax.experimental import pallas as pl
from jax.experimental.pallas import tpu as pltpu
from jax.sharding import PartitionSpec as P

TILE = 128
SPAN = 256
FEAT = 512
PER_ROW = 6
SLOTS = 192
CHUNK = 6
STEP = 4
WIDE = 384
PART = 64
HALF_ROWS = 8 * SPAN
BF16 = jnp.bfloat16
F32 = jnp.float32
SMEM = pl.BlockSpec(memory_space=pltpu.SMEM)
VMEM = pl.BlockSpec(memory_space=pltpu.VMEM)
DISTANCE = (0, 3, 1, 2)


def flat(x, y, z, core):
    return ((z % 2) * 4 + y % 4) * 16 + (x % 4) * 4 + (z // 2) * 2 + core


def permute(value, step):
    pairs = [
        (flat(x, y, z, c), flat(*step(x, y, z, c)))
        for x in range(4)
        for y in range(4)
        for z in range(4)
        for c in range(2)
    ]
    return lax.ppermute(value, ("row", "col"), pairs)


def to_core(x, y, z, c):
    return x, y, z, 1 - c


def ring(k):
    return lambda x, y, z, c: (x, y + k, z, c) if c == 0 else (x + k, y, z, c)


def to_z(x, y, z, c):
    return x, y, z ^ (1 if c == 0 else 2), c


def cross_ring(k):
    return lambda x, y, z, c: (x + k, y, z, c) if c == 0 else (x, y + k, z, c)


def along_z(k):
    return lambda x, y, z, c: (x, y, (z + k) % 4, c)


def rows(first, count):
    return pl.ds(pl.multiple_of(first, count), count)


def block(i):
    return rows(i * TILE, TILE)


def ring_place(distance):
    return jnp.where(distance == 0, 0, jnp.where(distance == 3, 1, distance + 1))


def coordinates():
    row, col = lax.axis_index("row"), lax.axis_index("col")
    return col // 4, row % 4, row // 4, (col // 2) % 2, col % 2


def part_at(core, place):
    x, y = coordinates()[:2]
    return (jnp.where(core == 0, y, x) + DISTANCE[place]) % 4


def panel_place(place):
    partner = 1 - (place >> 2)
    return jnp.where((place & 3) == 0, partner, 1 + (place & 3) + 3 * partner)


def lists_kernel(coords, count, lists):
    my_x, my_y, my_near, my_far, my_core = coordinates()
    live = count[0, 0]
    sublane = lax.broadcasted_iota(jnp.int32, (SLOTS, SLOTS), 0)
    lane = lax.broadcasted_iota(jnp.int32, (SLOTS, SLOTS), 1)
    wide = lax.broadcasted_iota(jnp.int32, (SLOTS, WIDE), 1)
    same = sublane == lane

    def picked(mask, value):
        return jnp.where(mask, value, 0.0)

    def column(line):
        return jnp.sum(picked(same, line.astype(F32)), axis=1, keepdims=True).astype(jnp.int32)

    row_line, col_line = coords[0:1, :], coords[1:2, :]
    a, b = column(row_line), column(col_line)
    a_owner, b_owner = a >> 1, b >> 1
    a_place = (1 - (((a_owner >> 1) & 1) ^ my_far)) * 4 + ring_place(((a_owner >> 2) - my_x) & 3)
    b_place = (1 - ((b_owner >> 2) ^ my_near)) * 4 + ring_place(((b_owner & 3) - my_y) & 3)
    a_from, b_from = panel_place(a_place), panel_place(b_place)
    a_tile = a_place * 4 + (a_owner & 1) * 2 + (a & 1)
    b_tile = b_place * 2 + (b & 1)
    a_source = a_from * 4 + (a_owner & 1) * 2 + (a & 1) + (1 - my_core) * 32
    b_source = b_from * 4 + my_core * 2 + (b & 1) + my_core * 32
    slot = sublane[:, 0:1]
    is_live = slot < live

    row_rank = jnp.sum(picked((a == row_line) & (lane < sublane), 1.0), axis=1, keepdims=True).astype(jnp.int32)
    at_row = wide == a_tile * PER_ROW + row_rank
    named = jnp.where(is_live, slot, -1).astype(F32)
    lists[0:1, :] = jnp.sum(picked(at_row, named), axis=0, keepdims=True).astype(jnp.int32)
    lists[1:2, :] = jnp.sum(picked(at_row, b_source.astype(F32)), axis=0, keepdims=True).astype(jnp.int32)

    earlier = (b == col_line) & (lane < sublane) & (lane < live)
    col_rank = jnp.sum(picked(earlier, 1.0), axis=1, keepdims=True).astype(jnp.int32)
    filled = jnp.sum(picked((b_tile == wide) & is_live, 1.0), axis=0, keepdims=True).astype(jnp.int32)
    chunks = ((filled + (CHUNK - 1)) * 43) >> 8
    used = jnp.sum(chunks.astype(F32), axis=1, keepdims=True).astype(jnp.int32)
    base = jnp.sum(picked(wide < b_tile, chunks.astype(F32)), axis=1, keepdims=True).astype(jnp.int32)
    which = (col_rank * 43) >> 8
    chunk = base + which
    place = col_rank - which * CHUNK
    at_chunk = (wide == chunk * CHUNK + place) & is_live
    opens = (wide == chunk) & is_live & (place == 0)
    lists[2:3, :] = jnp.sum(picked(at_chunk, (slot + 1).astype(F32)), axis=0, keepdims=True).astype(jnp.int32) - 1
    lists[3:4, :] = jnp.sum(picked(at_chunk, a_source.astype(F32)), axis=0, keepdims=True).astype(jnp.int32)
    lists[4:5, :] = jnp.sum(picked(opens, b_tile.astype(F32)), axis=0, keepdims=True).astype(jnp.int32)
    lists[5:6, :] = jnp.broadcast_to((used + (STEP - 1)) >> 2, (1, WIDE))
    lists[6:8, :] = jnp.zeros((2, WIDE), jnp.int32)


def make_lists(coords, count):
    return pl.pallas_call(
        lists_kernel,
        out_shape=jax.ShapeDtypeStruct((8, WIDE), jnp.int32),
        in_specs=[VMEM, SMEM],
        out_specs=VMEM,
        compiler_params=pltpu.CompilerParams(vmem_limit_bytes=12 * 2**20),
    )(coords, count)


def live_tile(values, slot):
    tile = values[jnp.maximum(slot, 0)]
    return jnp.where(slot >= 0, tile, jnp.zeros_like(tile))


def backward_kernel(lists, values, panels, far, near, term_keep, term_send, total, whole, term):
    core = coordinates()[4]
    total[...] = jnp.zeros_like(total)

    def chunk_step(q, carry):
        products = []
        for k in range(STEP):
            first = (q * STEP + k) * CHUNK
            tiles = [live_tile(values, lists[2, first + i]) for i in range(CHUNK)]
            source = [panels[block(lists[3, first + i]), :] for i in range(CHUNK)]
            products.append(
                lax.dot_general(
                    jnp.concatenate(tiles, axis=0),
                    jnp.concatenate(source, axis=0),
                    (((0,), (0,)), ((), ())),
                    preferred_element_type=F32,
                )
            )
        for k in range(STEP):
            total[block(lists[4, q * STEP + k]), :] += products[k]
        return carry

    lax.fori_loop(0, lists[5, 0], chunk_step, 0)
    whole[...] = total[...].astype(BF16)
    for half, target in ((0, far), (1, near)):
        for q in range(4):
            from_here = (half * 4 + q) * SPAN
            target[rows(q * 2 * SPAN + core * SPAN, SPAN), :] = whole[from_here : from_here + SPAN, :]
            target[rows(q * 2 * SPAN + (1 - core) * SPAN, SPAN), :] = jnp.zeros((SPAN, FEAT), BF16)
    start = core * 16 * SPAN + core * SPAN
    feats = jnp.concatenate([panels[rows(start + q * 2 * SPAN, SPAN), :] for q in (1, 5, 6, 7, 0, 2, 3, 4)], axis=0)
    term[...] = lax.dot_general(
        feats, whole[...], (((0,), (0,)), ((), ())), preferred_element_type=F32
    ).astype(BF16)
    for place in range(4):
        for target, side in ((term_keep, core), (term_send, 1 - core)):
            first = side * SPAN + part_at(side, place) * PART
            target[place * PART : (place + 1) * PART, :] = term[rows(first, PART), :]


def forward_kernel(half, lists, values, panels, back, keep, send, rows_out, sems):
    core = coordinates()[4]

    def move(source, target, sem):
        return pltpu.make_async_copy(source, target, sem)

    @pl.when(core == half)
    def _():
        move(back, keep, sems.at[0]).start()

    @pl.when(core == 1 - half)
    def _():
        move(back, send, sems.at[0]).start()

    for q in range(16 // STEP):
        here = pl.ds(q * STEP * TILE, STEP * TILE)
        for k in range(STEP):
            tile = q * STEP + k
            first = (half * 16 + tile) * PER_ROW
            tiles = [live_tile(values, lists[0, first + i]) for i in range(PER_ROW)]
            source = [panels[block(lists[1, first + i]), :] for i in range(PER_ROW)]
            rows_out[tile * TILE : (tile + 1) * TILE, :] = jnp.dot(
                jnp.concatenate(tiles, axis=1), jnp.concatenate(source, axis=0), preferred_element_type=F32
            ).astype(BF16)

        @pl.when(core == half)
        def _():
            move(rows_out.at[here], send.at[here], sems.at[1 + q]).start()

        @pl.when(core == 1 - half)
        def _():
            move(rows_out.at[here], keep.at[here], sems.at[1 + q]).start()

    move(back, keep, sems.at[0]).wait()
    for q in range(16 // STEP):
        here = pl.ds(q * STEP * TILE, STEP * TILE)
        move(rows_out.at[here], send.at[here], sems.at[1 + q]).wait()


def shape(n, dtype=BF16):
    return jax.ShapeDtypeStruct((n, FEAT), dtype)


def backward_sums(lists, values, panels):
    return pl.pallas_call(
        backward_kernel,
        out_shape=(shape(HALF_ROWS), shape(HALF_ROWS), shape(SPAN), shape(SPAN)),
        in_specs=[SMEM, VMEM, VMEM],
        out_specs=[VMEM] * 4,
        scratch_shapes=[
            pltpu.VMEM((8 * SPAN, FEAT), F32),
            pltpu.VMEM((8 * SPAN, FEAT), BF16),
            pltpu.VMEM((FEAT, FEAT), BF16),
        ],
        compiler_params=pltpu.CompilerParams(vmem_limit_bytes=12 * 2**20),
    )(lists, values, panels)


def forward_sums(half, lists, values, panels, back):
    return pl.pallas_call(
        functools.partial(forward_kernel, half),
        out_shape=(shape(HALF_ROWS), shape(HALF_ROWS)),
        in_specs=[SMEM, VMEM, VMEM, VMEM],
        out_specs=[VMEM] * 2,
        scratch_shapes=[pltpu.VMEM((HALF_ROWS, FEAT), BF16), pltpu.SemaphoreType.DMA((5,))],
        compiler_params=pltpu.CompilerParams(vmem_limit_bytes=8 * 2**20),
    )(lists, values, panels, back)


def finish_kernel(final, got, weight, output, grad):
    core = coordinates()[4]

    def both(summed, agg):
        output[...] = jnp.dot(summed, weight[...], preferred_element_type=F32).astype(BF16)
        grad[...] = lax.dot_general(
            agg, weight[...], (((1,), (1,)), ((), ())), preferred_element_type=F32
        ).astype(BF16)

    @pl.when(core == 0)
    def _():
        both(final[0:SPAN, :], got[...])

    @pl.when(core == 1)
    def _():
        both(got[...], final[SPAN : 2 * SPAN, :])


def finish(final, got, weight):
    return pl.pallas_call(
        finish_kernel,
        out_shape=(shape(SPAN), shape(SPAN)),
        in_specs=[VMEM] * 3,
        out_specs=(VMEM, VMEM),
        compiler_params=pltpu.CompilerParams(vmem_limit_bytes=8 * 2**20),
    )(final, got, weight)


def place_kernel(scale, mine, other, grad):
    core = coordinates()[4]
    for place in range(4):
        for source, side in ((mine, core), (other, 1 - core)):
            first = side * SPAN + part_at(side, place) * PART
            grad[rows(first, PART), :] = source[place * PART : (place + 1) * PART, :].astype(F32) * scale


def place_parts(scale, mine, other):
    return pl.pallas_call(
        functools.partial(place_kernel, scale),
        out_shape=shape(FEAT, F32),
        in_specs=[VMEM, VMEM],
        out_specs=VMEM,
        compiler_params=pltpu.CompilerParams(vmem_limit_bytes=8 * 2**20),
    )(mine, other)


def stack(*parts):
    return jnp.concatenate(parts, axis=0)


def add(*parts):
    total = parts[0].astype(F32)
    for part in parts[1:]:
        total = total + part.astype(F32)
    return total.astype(BF16)


def ring_gather(own, step):
    opposite = permute(own, step(2))
    return own, permute(own, step(1)), permute(own, step(-1)), opposite


def ring_sum(pieces, step):
    own, before, after, opposite = pieces
    opposite = permute(opposite, step(2))
    return own, permute(after, step(1)), permute(before, step(-1)), opposite


def split(whole, size):
    return [whole[i * size : (i + 1) * size] for i in range(4)]


def per_device(features, weight, cotangent, tile_coords, tile_values, tile_count):
    values = tile_values[0, 0]
    lists = make_lists(jnp.transpose(tile_coords[0, 0]), tile_count)
    first = lax.axis_index("col") % 2 == 0
    other_features, other_cotangent = permute(features, to_core), permute(cotangent, to_core)
    all_features = jnp.where(first, stack(features, other_features), stack(other_features, features))
    all_cotangent = jnp.where(first, stack(cotangent, other_cotangent), stack(other_cotangent, cotangent))
    own = jnp.where(first, all_features, all_cotangent)
    other_own = jnp.where(first, all_cotangent, all_features)
    from_z = permute(own, to_z)
    near = list(ring_gather(own, ring))
    before, after, opposite = near[1:]
    from_z, opposite, lists = lax.optimization_barrier((from_z, opposite, lists))
    far = ring_gather(from_z, ring)[1:]
    ringed = stack(from_z, before, after, opposite, *far)
    panels = stack(own, ringed, other_own, permute(ringed, to_core))

    back_far, back_near, term_keep, term_send = backward_sums(lists, values, panels)
    part = add(term_keep, permute(term_send, to_core))
    keep_far, send_far = forward_sums(0, lists, values, panels, back_far)
    sum_far = add(keep_far, permute(send_far, to_core))
    keep_near, send_near = forward_sums(1, lists, values, panels, back_near)
    send_near, part = lax.optimization_barrier((send_near, part))
    sum_near = add(keep_near, permute(send_near, to_core))
    far = [stack(*both) for both in zip(split(sum_far, 2 * SPAN), split(part, PART))]
    far = add(*ring_sum(far, ring))
    far, part = far[: 2 * SPAN], far[2 * SPAN :]
    near = add(*ring_sum([stack(piece, part) for piece in split(sum_near, 2 * SPAN)], cross_ring))
    near, part = near[: 2 * SPAN], near[2 * SPAN :]
    passed = permute(permute(far, to_z), to_core)
    part = add(*ring_gather(part, along_z))
    mine = stack(*ring_gather(part, ring))
    other = permute(mine, to_core)
    final = add(near, passed)
    got = permute(jnp.where(first, final[SPAN:], final[:SPAN]), to_core)
    output, features_grad = finish(final, got, weight)
    other, output, features_grad = lax.optimization_barrier((other, output, features_grad))
    nodes = lax.axis_size("row") * lax.axis_size("col") * SPAN
    weight_grad = place_parts(nodes ** (-0.5), mine, other)
    return output, features_grad, weight_grad


def solution(mesh):
    return jax.shard_map(
        per_device,
        mesh=mesh,
        in_specs=(
            P(("row", "col"), None),
            P(),
            P(("row", "col"), None),
            P("row", "col", None, None),
            P("row", "col", None, None, None),
            P("row", "col"),
        ),
        out_specs=(P(("row", "col"), None), P(("row", "col"), None), P()),
        check_vma=False,
    )
```

```python
import functools

import jax
import jax.numpy as jnp
from jax import lax
from jax.experimental import pallas as pl
from jax.experimental.pallas import tpu as pltpu
from jax.sharding import PartitionSpec as P

TILE = 128
SPAN = 256
FEAT = 512
PER_ROW = 6
SLOTS = 192
CHUNK = 6
STEP = 4
WIDE = 384
PART = 64
HALF_ROWS = 8 * SPAN
BF16 = jnp.bfloat16
F32 = jnp.float32
SMEM = pl.BlockSpec(memory_space=pltpu.SMEM)
VMEM = pl.BlockSpec(memory_space=pltpu.VMEM)
DISTANCE = (0, 3, 1, 2)


def flat(x, y, z, core):
    return ((z % 2) * 4 + y % 4) * 16 + (x % 4) * 4 + (z // 2) * 2 + core


def permute(value, step):
    pairs = [
        (flat(x, y, z, c), flat(*step(x, y, z, c)))
        for x in range(4)
        for y in range(4)
        for z in range(4)
        for c in range(2)
    ]
    return lax.ppermute(value, ("row", "col"), pairs)


def to_core(x, y, z, c):
    return x, y, z, 1 - c


def ring(k):
    return lambda x, y, z, c: (x, y + k, z, c) if c == 0 else (x + k, y, z, c)


def to_z(x, y, z, c):
    return x, y, z ^ (1 if c == 0 else 2), c


def cross_ring(k):
    return lambda x, y, z, c: (x + k, y, z, c) if c == 0 else (x, y + k, z, c)


def along_z(k):
    return lambda x, y, z, c: (x, y, (z + k) % 4, c)


def rows(first, count):
    return pl.ds(pl.multiple_of(first, count), count)


def block(i):
    return rows(i * TILE, TILE)


def ring_place(distance):
    return jnp.where(distance == 0, 0, jnp.where(distance == 3, 1, distance + 1))


def coordinates():
    row, col = lax.axis_index("row"), lax.axis_index("col")
    return col // 4, row % 4, row // 4, (col // 2) % 2, col % 2


def part_at(core, place):
    x, y = coordinates()[:2]
    return (jnp.where(core == 0, y, x) + DISTANCE[place]) % 4


def panel_place(place):
    partner = 1 - (place >> 2)
    return jnp.where((place & 3) == 0, partner, 1 + (place & 3) + 3 * partner)


def lists_kernel(coords, count, lists):
    my_x, my_y, my_near, my_far, my_core = coordinates()
    live = count[0, 0]
    sublane = lax.broadcasted_iota(jnp.int32, (SLOTS, SLOTS), 0)
    lane = lax.broadcasted_iota(jnp.int32, (SLOTS, SLOTS), 1)
    wide = lax.broadcasted_iota(jnp.int32, (SLOTS, WIDE), 1)
    same = sublane == lane

    def picked(mask, value):
        return jnp.where(mask, value, 0.0)

    def column(line):
        return jnp.sum(picked(same, line.astype(F32)), axis=1, keepdims=True).astype(jnp.int32)

    row_line, col_line = coords[0:1, :], coords[1:2, :]
    a, b = column(row_line), column(col_line)
    a_owner, b_owner = a >> 1, b >> 1
    a_place = (1 - (((a_owner >> 1) & 1) ^ my_far)) * 4 + ring_place(((a_owner >> 2) - my_x) & 3)
    b_place = (1 - ((b_owner >> 2) ^ my_near)) * 4 + ring_place(((b_owner & 3) - my_y) & 3)
    a_from, b_from = panel_place(a_place), panel_place(b_place)
    a_tile = a_place * 4 + (a_owner & 1) * 2 + (a & 1)
    b_tile = b_place * 2 + (b & 1)
    a_source = a_from * 4 + (a_owner & 1) * 2 + (a & 1) + (1 - my_core) * 32
    b_source = b_from * 4 + my_core * 2 + (b & 1) + my_core * 32
    slot = sublane[:, 0:1]
    is_live = slot < live

    row_rank = jnp.sum(picked((a == row_line) & (lane < sublane), 1.0), axis=1, keepdims=True).astype(jnp.int32)
    at_row = wide == a_tile * PER_ROW + row_rank
    named = jnp.where(is_live, slot, -1).astype(F32)
    lists[0:1, :] = jnp.sum(picked(at_row, named), axis=0, keepdims=True).astype(jnp.int32)
    lists[1:2, :] = jnp.sum(picked(at_row, b_source.astype(F32)), axis=0, keepdims=True).astype(jnp.int32)

    earlier = (b == col_line) & (lane < sublane) & (lane < live)
    col_rank = jnp.sum(picked(earlier, 1.0), axis=1, keepdims=True).astype(jnp.int32)
    filled = jnp.sum(picked((b_tile == wide) & is_live, 1.0), axis=0, keepdims=True).astype(jnp.int32)
    chunks = ((filled + (CHUNK - 1)) * 43) >> 8
    used = jnp.sum(chunks.astype(F32), axis=1, keepdims=True).astype(jnp.int32)
    base = jnp.sum(picked(wide < b_tile, chunks.astype(F32)), axis=1, keepdims=True).astype(jnp.int32)
    which = (col_rank * 43) >> 8
    chunk = base + which
    place = col_rank - which * CHUNK
    at_chunk = (wide == chunk * CHUNK + place) & is_live
    opens = (wide == chunk) & is_live & (place == 0)
    lists[2:3, :] = jnp.sum(picked(at_chunk, (slot + 1).astype(F32)), axis=0, keepdims=True).astype(jnp.int32) - 1
    lists[3:4, :] = jnp.sum(picked(at_chunk, a_source.astype(F32)), axis=0, keepdims=True).astype(jnp.int32)
    lists[4:5, :] = jnp.sum(picked(opens, b_tile.astype(F32)), axis=0, keepdims=True).astype(jnp.int32)
    lists[5:6, :] = jnp.broadcast_to((used + (STEP - 1)) >> 2, (1, WIDE))
    lists[6:8, :] = jnp.zeros((2, WIDE), jnp.int32)


def make_lists(coords, count):
    return pl.pallas_call(
        lists_kernel,
        out_shape=jax.ShapeDtypeStruct((8, WIDE), jnp.int32),
        in_specs=[VMEM, SMEM],
        out_specs=VMEM,
        compiler_params=pltpu.CompilerParams(vmem_limit_bytes=12 * 2**20),
    )(coords, count)


def live_tile(values, slot):
    tile = values[jnp.maximum(slot, 0)]
    return jnp.where(slot >= 0, tile, jnp.zeros_like(tile))


def backward_kernel(lists, values, panels, far, near, term_keep, term_send, total, whole, term):
    core = coordinates()[4]
    total[...] = jnp.zeros_like(total)

    def chunk_step(q, carry):
        products = []
        for k in range(STEP):
            first = (q * STEP + k) * CHUNK
            tiles = [live_tile(values, lists[2, first + i]) for i in range(CHUNK)]
            source = [panels[block(lists[3, first + i]), :] for i in range(CHUNK)]
            products.append(
                lax.dot_general(
                    jnp.concatenate(tiles, axis=0),
                    jnp.concatenate(source, axis=0),
                    (((0,), (0,)), ((), ())),
                    preferred_element_type=F32,
                )
            )
        for k in range(STEP):
            total[block(lists[4, q * STEP + k]), :] += products[k]
        return carry

    lax.fori_loop(0, lists[5, 0], chunk_step, 0)
    whole[...] = total[...].astype(BF16)
    for half, target in ((0, far), (1, near)):
        for q in range(4):
            from_here = (half * 4 + q) * SPAN
            target[rows(q * 2 * SPAN + core * SPAN, SPAN), :] = whole[from_here : from_here + SPAN, :]
            target[rows(q * 2 * SPAN + (1 - core) * SPAN, SPAN), :] = jnp.zeros((SPAN, FEAT), BF16)
    start = core * 16 * SPAN + core * SPAN
    feats = jnp.concatenate([panels[rows(start + q * 2 * SPAN, SPAN), :] for q in (1, 5, 6, 7, 0, 2, 3, 4)], axis=0)
    term[...] = lax.dot_general(
        feats, whole[...], (((0,), (0,)), ((), ())), preferred_element_type=F32
    ).astype(BF16)
    for place in range(4):
        for target, side in ((term_keep, core), (term_send, 1 - core)):
            first = side * SPAN + part_at(side, place) * PART
            target[place * PART : (place + 1) * PART, :] = term[rows(first, PART), :]


def forward_kernel(half, lists, values, panels, back, keep, send, rows_out, sems):
    core = coordinates()[4]

    def move(source, target, sem):
        return pltpu.make_async_copy(source, target, sem)

    @pl.when(core == half)
    def _():
        move(back, keep, sems.at[0]).start()

    @pl.when(core == 1 - half)
    def _():
        move(back, send, sems.at[0]).start()

    for q in range(16 // STEP):
        here = pl.ds(q * STEP * TILE, STEP * TILE)
        for k in range(STEP):
            tile = q * STEP + k
            first = (half * 16 + tile) * PER_ROW
            tiles = [live_tile(values, lists[0, first + i]) for i in range(PER_ROW)]
            source = [panels[block(lists[1, first + i]), :] for i in range(PER_ROW)]
            rows_out[tile * TILE : (tile + 1) * TILE, :] = jnp.dot(
                jnp.concatenate(tiles, axis=1), jnp.concatenate(source, axis=0), preferred_element_type=F32
            ).astype(BF16)

        @pl.when(core == half)
        def _():
            move(rows_out.at[here], send.at[here], sems.at[1 + q]).start()

        @pl.when(core == 1 - half)
        def _():
            move(rows_out.at[here], keep.at[here], sems.at[1 + q]).start()

    move(back, keep, sems.at[0]).wait()
    for q in range(16 // STEP):
        here = pl.ds(q * STEP * TILE, STEP * TILE)
        move(rows_out.at[here], send.at[here], sems.at[1 + q]).wait()


def shape(n, dtype=BF16):
    return jax.ShapeDtypeStruct((n, FEAT), dtype)


def backward_sums(lists, values, panels):
    return pl.pallas_call(
        backward_kernel,
        out_shape=(shape(HALF_ROWS), shape(HALF_ROWS), shape(SPAN), shape(SPAN)),
        in_specs=[SMEM, VMEM, VMEM],
        out_specs=[VMEM] * 4,
        scratch_shapes=[
            pltpu.VMEM((8 * SPAN, FEAT), F32),
            pltpu.VMEM((8 * SPAN, FEAT), BF16),
            pltpu.VMEM((FEAT, FEAT), BF16),
        ],
        compiler_params=pltpu.CompilerParams(vmem_limit_bytes=12 * 2**20),
    )(lists, values, panels)


def forward_sums(half, lists, values, panels, back):
    return pl.pallas_call(
        functools.partial(forward_kernel, half),
        out_shape=(shape(HALF_ROWS), shape(HALF_ROWS)),
        in_specs=[SMEM, VMEM, VMEM, VMEM],
        out_specs=[VMEM] * 2,
        scratch_shapes=[pltpu.VMEM((HALF_ROWS, FEAT), BF16), pltpu.SemaphoreType.DMA((5,))],
        compiler_params=pltpu.CompilerParams(vmem_limit_bytes=8 * 2**20),
    )(lists, values, panels, back)


def finish_kernel(final, got, weight, output, grad):
    core = coordinates()[4]

    def both(summed, agg):
        output[...] = jnp.dot(summed, weight[...], preferred_element_type=F32).astype(BF16)
        grad[...] = lax.dot_general(
            agg, weight[...], (((1,), (1,)), ((), ())), preferred_element_type=F32
        ).astype(BF16)

    @pl.when(core == 0)
    def _():
        both(final[0:SPAN, :], got[...])

    @pl.when(core == 1)
    def _():
        both(got[...], final[SPAN : 2 * SPAN, :])


def finish(final, got, weight):
    return pl.pallas_call(
        finish_kernel,
        out_shape=(shape(SPAN), shape(SPAN)),
        in_specs=[VMEM] * 3,
        out_specs=(VMEM, VMEM),
        compiler_params=pltpu.CompilerParams(vmem_limit_bytes=8 * 2**20),
    )(final, got, weight)


def place_kernel(scale, mine, other, grad):
    core = coordinates()[4]
    for place in range(4):
        for source, side in ((mine, core), (other, 1 - core)):
            first = side * SPAN + part_at(side, place) * PART
            grad[rows(first, PART), :] = source[place * PART : (place + 1) * PART, :].astype(F32) * scale


def place_parts(scale, mine, other):
    return pl.pallas_call(
        functools.partial(place_kernel, scale),
        out_shape=shape(FEAT, F32),
        in_specs=[VMEM, VMEM],
        out_specs=VMEM,
        compiler_params=pltpu.CompilerParams(vmem_limit_bytes=8 * 2**20),
    )(mine, other)


def stack(*parts):
    return jnp.concatenate(parts, axis=0)


def add(*parts):
    total = parts[0].astype(F32)
    for part in parts[1:]:
        total = total + part.astype(F32)
    return total.astype(BF16)


def ring_gather(own, step):
    opposite = permute(own, step(2))
    return own, permute(own, step(1)), permute(own, step(-1)), opposite


def ring_sum(pieces, step):
    own, before, after, opposite = pieces
    opposite = permute(opposite, step(2))
    return own, permute(after, step(1)), permute(before, step(-1)), opposite


def split(whole, size):
    return [whole[i * size : (i + 1) * size] for i in range(4)]


def per_device(features, weight, cotangent, tile_coords, tile_values, tile_count):
    values = tile_values[0, 0]
    lists = make_lists(jnp.transpose(tile_coords[0, 0]), tile_count)
    first = lax.axis_index("col") % 2 == 0
    other_features, other_cotangent = permute(features, to_core), permute(cotangent, to_core)
    all_features = jnp.where(first, stack(features, other_features), stack(other_features, features))
    all_cotangent = jnp.where(first, stack(cotangent, other_cotangent), stack(other_cotangent, cotangent))
    own = jnp.where(first, all_features, all_cotangent)
    other_own = jnp.where(first, all_cotangent, all_features)
    from_z = permute(own, to_z)
    near = list(ring_gather(own, ring))
    before, after, opposite = near[1:]
    from_z, opposite, lists = lax.optimization_barrier((from_z, opposite, lists))
    far = ring_gather(from_z, ring)[1:]
    ringed = stack(from_z, before, after, opposite, *far)
    panels = stack(own, ringed, other_own, permute(ringed, to_core))

    back_far, back_near, term_keep, term_send = backward_sums(lists, values, panels)
    part = add(term_keep, permute(term_send, to_core))
    keep_far, send_far = forward_sums(0, lists, values, panels, back_far)
    sum_far = add(keep_far, permute(send_far, to_core))
    keep_near, send_near = forward_sums(1, lists, values, panels, back_near)
    send_near, part = lax.optimization_barrier((send_near, part))
    sum_near = add(keep_near, permute(send_near, to_core))
    far = [stack(*both) for both in zip(split(sum_far, 2 * SPAN), split(part, PART))]
    far = add(*ring_sum(far, ring))
    far, part = far[: 2 * SPAN], far[2 * SPAN :]
    near = add(*ring_sum([stack(piece, part) for piece in split(sum_near, 2 * SPAN)], cross_ring))
    near, part = near[: 2 * SPAN], near[2 * SPAN :]
    passed = permute(far, to_z)
    around = ring_gather(part, along_z)
    passed, *around = lax.optimization_barrier((passed, *around))
    part = add(*around)
    passed = permute(passed, to_core)
    mine = stack(*ring_gather(part, ring))
    other = permute(mine, to_core)
    final = add(near, passed)
    got = permute(jnp.where(first, final[SPAN:], final[:SPAN]), to_core)
    output, features_grad = finish(final, got, weight)
    other, output, features_grad = lax.optimization_barrier((other, output, features_grad))
    nodes = lax.axis_size("row") * lax.axis_size("col") * SPAN
    weight_grad = place_parts(nodes ** (-0.5), mine, other)
    return output, features_grad, weight_grad


def solution(mesh):
    return jax.shard_map(
        per_device,
        mesh=mesh,
        in_specs=(
            P(("row", "col"), None),
            P(),
            P(("row", "col"), None),
            P("row", "col", None, None),
            P("row", "col", None, None, None),
            P("row", "col"),
        ),
        out_specs=(P(("row", "col"), None), P(("row", "col"), None), P()),
        check_vma=False,
    )
```
